32 devices in a mesh: groups: 2 (over y), tensor: 4 (over z), dp: 2 (over x), seq: 2 (over core).
Axes of the slice: x: 2, y: 2, z: 4, core: 2. Of those that a mesh axis runs over, the one named last changes fastest.
Arguments:
- tokens: bfloat16 [8, 512, 4096], P(('groups', 'dp', 'seq'), 'tensor'), parts along dimension 0, may hold values from -6 to 6
- grad_out: bfloat16 [8, 512, 4096], P(('groups', 'dp', 'seq'), 'tensor'), parts along dimension 0, may hold values from -6 to 6
- up_blocks: bfloat16 [4, 2, 256, 256], P('tensor'), may hold values from -0.375 to 0.375
- down_blocks: bfloat16 [4, 2, 256, 256], P('tensor'), may hold values from -0.375 to 0.375
- pairs: int32 [4, 2, 2], replicated, may hold values from 0 to 15, as said below
- live: int32 [4], replicated, may hold values from 1 to 2, as said below
- left_factor: bfloat16 [4096, 16], replicated, may hold values from -0.09375 to 0.09375
- right_factor: bfloat16 [16, 4096], P(None, 'tensor'), may hold values from -1.5 to 1.5
Outputs:
- grad_tokens: bfloat16 [8, 512, 4096], P(('groups', 'dp', 'seq'), 'tensor'), parts along dimension 0
- grad_up: float32 [8, 2, 256, 256], P(('groups', 'tensor'), None, ('dp', 'seq')), parts along dimension 0
- grad_down: float32 [8, 2, 256, 256], P(('groups', 'tensor'), None, ('dp', 'seq')), parts along dimension 0
- grad_left: float32 [8192, 16], P(('groups', 'tensor'), ('dp', 'seq')), parts along dimension 0
- grad_right: float32 [32, 4096], P(('groups', 'dp', 'seq'), 'tensor'), parts along dimension 0
The draws below stay inside these ranges and needn't reach their ends.
There are 2 independent parts, one for each index of `groups`. The reference program is written for one: setup_inputs(seed, part) draws one part's arguments, and reference() takes and returns one part's arrays. A program takes and returns all parts, laid end to end along the dimension named above; an argument that names none is the same for every part. Nothing has to cross between parts.
Inputs may be any that keep to these rules, and one draw needn't show every extreme that they name: pairs[p, s, 0] is a feature row block in 0 .. 15 and pairs[p, s, 1] a column block within the panel in 0 .. 3. Each panel has 1 or 2 live slots; some panel has all 2 live.
All inputs are finite; a program needn't handle non-finite values.
Results may differ from the reference program's by a relative error of at most 0.006.
Values may be sent and summed in bfloat16 or wider, within the bound.
No kernel may reach another device: no remote copies, remote signals or barrier semaphores. Data moves between devices by JAX's collectives and lax.ppermute only.
A program may use at most 128 MiB of HBM per device.

```python
import jax
import jax.numpy as jnp
from jax import lax

D = 4096
BLK = 256
FF_DEV = 1024
SLOTS = 2
RANK = 16
PANELS = 4
FF = 4096
TOKS = 512
REPL = 4


def draw_pairs(key, part):
    key = jax.random.fold_in(key, 11)
    nblocks = D // BLK
    levels = nblocks.bit_length() - 1
    ncols = FF_DEV // BLK
    key_col, key_lvl = jax.random.split(key)
    cols = jax.random.randint(key_col, (PANELS, SLOTS), 0, ncols)
    first = jax.random.randint(key_lvl, (PANELS, 1), 0, levels)
    lvl = (first + jnp.arange(SLOTS)[None, :]) % levels
    target = (nblocks - 2) // ncols
    cols = cols.at[target, 0].set((nblocks - 2) % ncols)
    lvl = lvl.at[target, 0].set(0)
    cols = cols.at[0, 1].set(0)
    glob = jnp.arange(PANELS)[:, None] * ncols + cols
    rows = jnp.bitwise_xor(glob % nblocks, jnp.left_shift(1, lvl))
    return jnp.stack([rows, cols], axis=-1).astype(jnp.int32)


def draw_live(key, part):
    key = jax.random.fold_in(key, 23)
    key_a, key_b = jax.random.split(key)
    busy = jax.random.randint(key_a, (PANELS,), 0, 4) == 0
    counts = jnp.where(busy, SLOTS, 1)
    chosen = jax.random.randint(key_b, (), 0, PANELS)
    counts = counts.at[chosen].set(SLOTS)
    counts = counts.at[(chosen + 1) % PANELS].set(1)
    return counts.astype(jnp.int32)


def block_scale(key, dims, pieces, least, top_value):
    loudness = 1.0
    for dim, blocks in pieces:
        steps = jax.random.uniform(jax.random.fold_in(jax.random.fold_in(key, 6), dim), (blocks,), jnp.float32, least / len(pieces), top_value / len(pieces))
        loudness = loudness * jnp.repeat(jnp.exp(steps), dims[dim] // blocks).reshape((-1,) + (1,) * (len(dims) - 1 - dim))
    return loudness


def gaussian(own_key, extent, deviation, most, shards=(), held_as=jnp.bfloat16):
    level = block_scale(own_key, extent, shards, -0.22, 0.18) if shards else 1.0
    entries = jax.random.normal(own_key, extent, jnp.float32) * deviation * level
    return jnp.minimum(jnp.maximum(entries, -most), most).astype(held_as)


def setup_inputs(seed: int = 0, part: int = 0) -> dict:
    seeds = jax.random.split(jax.random.key(seed), 9)
    own_keys = jax.random.split(jax.random.fold_in(seeds[8], part), 9)
    tokens = gaussian(own_keys[0], (REPL, TOKS, D), 1.0, 6.0, ((0, 4), (1, 4)))
    grad_out = gaussian(own_keys[1], (REPL, TOKS, D), 1.0, 6.0, ((0, 4), (1, 4)))
    up_blocks = gaussian(seeds[2], (PANELS, SLOTS, BLK, BLK), BLK ** -0.5, 0.375, ((0, 4),))
    down_blocks = gaussian(seeds[3], (PANELS, SLOTS, BLK, BLK), BLK ** -0.5, 0.375, ((0, 4),))
    pairs = draw_pairs(jax.random.fold_in(seeds[8], 71), part)
    live = draw_live(jax.random.fold_in(seeds[8], 71), part)
    left_factor = gaussian(seeds[6], (D, RANK), D ** -0.5, 0.09375)
    right_factor = gaussian(seeds[7], (RANK, FF), RANK ** -0.5, 1.5, ((1, 4),))
    return {"tokens": tokens, "grad_out": grad_out, "up_blocks": up_blocks, "down_blocks": down_blocks, "pairs": pairs, "live": live, "left_factor": left_factor, "right_factor": right_factor}


def swish(value):
    return value * jax.nn.sigmoid(value)


def swish_slope(value):
    sig = jax.nn.sigmoid(value)
    return sig * (1.0 + value * (1.0 - sig))


def panel_pass(x_rows, dy_rows, factor, panel):
    up_p, down_p, pairs_p, live_p, right_p = panel
    pre = jnp.dot(factor, right_p, preferred_element_type=jnp.float32)

    def forward_slot(s, pre):
        row = pairs_p[s, 0].astype(jnp.int32)
        col = pairs_p[s, 1].astype(jnp.int32)
        piece = lax.dynamic_slice_in_dim(x_rows, row * BLK, BLK, 1)
        cur = lax.dynamic_slice_in_dim(pre, col * BLK, BLK, 1)
        new = cur + jnp.dot(piece, up_p[s], preferred_element_type=jnp.float32)
        return lax.dynamic_update_slice_in_dim(pre, new, col * BLK, 1)

    pre = lax.fori_loop(0, live_p, forward_slot, pre)
    act = pre.astype(jnp.bfloat16)

    def grad_slot(s, dh):
        row = pairs_p[s, 0].astype(jnp.int32)
        col = pairs_p[s, 1].astype(jnp.int32)
        piece = lax.dynamic_slice_in_dim(dy_rows, row * BLK, BLK, 1)
        cur = lax.dynamic_slice_in_dim(dh, col * BLK, BLK, 1)
        new = cur + jnp.dot(piece, down_p[s].T, preferred_element_type=jnp.float32)
        return lax.dynamic_update_slice_in_dim(dh, new, col * BLK, 1)

    dh = lax.fori_loop(0, live_p, grad_slot, jnp.zeros(pre.shape, jnp.float32))
    dact = (dh * swish_slope(act.astype(jnp.float32))).astype(jnp.bfloat16)
    g_term = jnp.dot(dact, right_p.T, preferred_element_type=jnp.float32)
    right_term = jnp.dot(factor.T, dact, preferred_element_type=jnp.float32)

    def back_slot(s, carry):
        dx_acc, gw_up, gw_down = carry
        row = pairs_p[s, 0].astype(jnp.int32)
        col = pairs_p[s, 1].astype(jnp.int32)
        xs = lax.dynamic_slice_in_dim(x_rows, row * BLK, BLK, 1)
        dys = lax.dynamic_slice_in_dim(dy_rows, row * BLK, BLK, 1)
        dslice = lax.dynamic_slice_in_dim(dact, col * BLK, BLK, 1)
        hid = swish(lax.dynamic_slice_in_dim(act, col * BLK, BLK, 1).astype(jnp.float32)).astype(jnp.bfloat16)
        gw_up = lax.dynamic_update_index_in_dim(gw_up, jnp.dot(xs.T, dslice, preferred_element_type=jnp.float32), s, 0)
        gw_down = lax.dynamic_update_index_in_dim(gw_down, jnp.dot(hid.T, dys, preferred_element_type=jnp.float32), s, 0)
        part = jnp.dot(dslice, up_p[s].T, preferred_element_type=jnp.float32).astype(jnp.bfloat16)
        part = lax.optimization_barrier(part).astype(jnp.float32)
        cur = lax.dynamic_slice_in_dim(dx_acc, row * BLK, BLK, 1)
        dx_acc = lax.dynamic_update_slice_in_dim(dx_acc, cur + part, row * BLK, 1)
        return dx_acc, gw_up, gw_down

    start = (jnp.zeros(x_rows.shape, jnp.float32), jnp.zeros((SLOTS, BLK, BLK), jnp.float32), jnp.zeros((SLOTS, BLK, BLK), jnp.float32))
    dx_part, gw_up, gw_down = lax.fori_loop(0, live_p, back_slot, start)
    return dx_part, g_term, gw_up, gw_down, right_term


def reference(tokens, grad_out, up_blocks, down_blocks, pairs, live, left_factor, right_factor):
    right_panels = right_factor.reshape(RANK, PANELS, FF_DEV).transpose(1, 0, 2)

    def replica_step(totals, inputs):
        x_rows, dy_rows = inputs
        factor = jnp.dot(x_rows, left_factor, preferred_element_type=jnp.float32).astype(jnp.bfloat16)

        def panel_step(carry, panel):
            dx_acc, g_acc = carry
            dx_part, g_term, gw_up, gw_down, right_term = panel_pass(x_rows, dy_rows, factor, panel)
            return (dx_acc + dx_part, g_acc + g_term), (gw_up, gw_down, right_term)

        start = (jnp.zeros(x_rows.shape, jnp.float32), jnp.zeros((x_rows.shape[0], RANK), jnp.float32))
        (dx_acc, g_acc), (gw_up, gw_down, right_terms) = lax.scan(panel_step, start, (up_blocks, down_blocks, pairs, live, right_panels))
        gfac = g_acc.astype(jnp.bfloat16)
        dx = (dx_acc + jnp.dot(gfac, left_factor.T, preferred_element_type=jnp.float32)).astype(jnp.bfloat16)
        left_term = jnp.dot(x_rows.T, gfac, preferred_element_type=jnp.float32)
        up_tot, down_tot, left_tot, right_tot = totals
        return (up_tot + gw_up, down_tot + gw_down, left_tot + left_term, right_tot + right_terms), dx

    zeros = (jnp.zeros((PANELS, SLOTS, BLK, BLK), jnp.float32), jnp.zeros((PANELS, SLOTS, BLK, BLK), jnp.float32), jnp.zeros((D, RANK), jnp.float32), jnp.zeros((PANELS, RANK, FF_DEV), jnp.float32))
    (grad_up, grad_down, grad_left, right_tot), grad_tokens = lax.scan(replica_step, zeros, (tokens, grad_out))
    grad_right = right_tot.transpose(1, 0, 2).reshape(RANK, PANELS * FF_DEV)
    return grad_tokens, grad_up, grad_down, grad_left, grad_right
```

```python
import functools

import jax
import jax.numpy as jnp
from jax import lax
from jax.experimental import pallas as pl
from jax.experimental.pallas import tpu as pltpu
from jax.sharding import PartitionSpec as P

BF = jnp.bfloat16
F32 = jnp.float32
VM = pltpu.VMEM


def dot(a, b, ca, cb):
    return lax.dot_general(a, b, (((ca,), (cb,)), ((), ())), preferred_element_type=F32)


def split_seq(value, ndp, nseq, here):
    rows = value.shape[0] // (ndp * nseq)
    v = [[value[(d * nseq + s) * rows : (d * nseq + s + 1) * rows] for d in range(ndp)] for s in range(nseq)]
    first, second = jnp.stack(v[0]), jnp.stack(v[1])
    return jnp.where(here == 0, first, second), jnp.where(here == 0, second, first)


def panel_math(ndp, nseq, shift, pairs, live, xcol, dycol, factor, up, down, right, keep, give, parts, gacc, rgrad):
    npan = lax.axis_size("tensor")
    here = lax.axis_index("seq")
    panel = lax.rem(lax.axis_index("tensor") + shift, npan)
    slots = parts.shape[0]
    blk = parts.shape[2]
    cols = [pairs[panel, s, 1] for s in range(slots)]
    alive = [s < live[panel] for s in range(slots)]
    fac = factor[...]
    block_up, block_down, rights = [], [], []
    for s in range(slots):
        block_up.append(dot(xcol[s], up(s), 1, 0))
        block_down.append(dot(dycol[s], down(s), 1, 1))
        rights.append(right(cols[s]))
    rgrad[...] = jnp.zeros(rgrad.shape, F32)
    gsum = None
    for s in range(slots):
        pre = dot(fac, rights[s], 1, 0)
        dh = jnp.zeros(pre.shape, F32)
        single = alive[s]
        for t in range(slots):
            same = jnp.logical_and(cols[t] == cols[s], alive[t])
            pre = pre + jnp.where(same, block_up[t], 0.0)
            dh = dh + jnp.where(same, block_down[t], 0.0)
            if t < s:
                single = jnp.logical_and(single, jnp.logical_not(same))
        act = pre.astype(BF).astype(F32)
        sig = jax.nn.sigmoid(act)
        hid = (act * sig).astype(BF)
        dpre = (dh * (sig * (1.0 + act * (1.0 - sig)))).astype(BF)
        once = jnp.where(single, dpre, jnp.zeros_like(dpre))
        term = dot(once, rights[s], 1, 1)
        gsum = term if gsum is None else gsum + term
        where = pl.ds(pl.multiple_of(cols[s] * blk, blk), blk)
        rgrad[:, where] = rgrad[:, where] + dot(fac, once, 0, 0)
        part = dot(dpre, up(s), 1, 1)
        parts[s] = jnp.where(alive[s], part, 0.0).astype(BF)
        gup = jnp.where(alive[s], dot(xcol[s], dpre, 0, 0), 0.0)
        gdown = jnp.where(alive[s], dot(hid, dycol[s], 0, 0), 0.0)
        for a, grad in ((0, gup), (1, gdown)):
            mine, other = split_seq(grad, ndp, nseq, here)
            keep[:, a, s] = mine.astype(keep.dtype)
            give[:, a, s] = other.astype(give.dtype)
    gacc[...] = gsum


def own_kernel(ndp, nseq, pairs, live, x, dy, left, up, down, right, xg, dyg, factor, keep, give, parts, gacc, rgrad):
    npan, slots, _, blk = xg.shape
    me = lax.axis_index("tensor")
    for k in range(npan):
        panel = lax.rem(me + k, npan)
        for s in range(slots):
            where = pl.ds(pl.multiple_of(pairs[panel, s, 0] * blk, blk), blk)
            xg[k, s] = x[:, where]
            dyg[k, s] = dy[:, where]
    factor[...] = dot(x[...], left[...], 1, 0).astype(BF)

    def right_block(c):
        return right[:, pl.ds(pl.multiple_of(c * blk, blk), blk)]

    panel_math(ndp, nseq, 0, pairs, live, xg.at[0], dyg.at[0], factor, lambda s: up[0, s], lambda s: down[0, s],
               right_block, keep, give, parts, gacc, rgrad)


def far_kernel(ndp, nseq, shift, pairs, live, xg, dyg, factor, near, far, keep, give, parts, gacc, rgrad, mats, rblk):
    blk = mats.shape[2]
    rank = rblk.shape[1]
    here, grp = lax.axis_index("seq"), lax.axis_index("groups")
    nseq_ = mats.shape[1]
    for src, c in ((near, here), (far, 1 - here)):
        for i, g in ((0, grp), (1, 1 - grp)):
            mats[g, c] = src[i, :blk]
            rblk[g * nseq_ + c] = src[i, blk : blk + rank]
    panel_math(ndp, nseq, shift, pairs, live, xg, dyg, factor, lambda s: mats[0, s], lambda s: mats[1, s],
               lambda c: rblk[c], keep, give, parts, gacc, rgrad)


def left_kernel(ndp, nseq, x, gacc, rgrad, gfac, keep, give):
    npan = gacc.shape[0]
    chunk = x.shape[1] // npan
    me, here = lax.axis_index("tensor"), lax.axis_index("seq")
    total = gacc[0]
    for k in range(1, npan):
        total = total + gacc[k]
    gf = total.astype(BF)
    gfac[...] = gf
    for k in range(npan):
        panel = lax.rem(me + k, npan)
        lg = dot(gf, x[:, pl.ds(pl.multiple_of(panel * chunk, chunk), chunk)], 0, 0)
        for value, lo in ((lg, 0), (rgrad[k], chunk)):
            mine, other = split_seq(value, ndp, nseq, here)
            width = value.shape[1]
            rows = mine.shape[1]
            for d in range(ndp):
                keep[k, d * rows : (d + 1) * rows, lo : lo + width] = mine[d]
                give[k, d * rows : (d + 1) * rows, lo : lo + width] = other[d]


def dx_kernel(pairs, live, left, gfac, parts, dx, acc):
    npan, slots, _, blk = parts.shape
    me = lax.axis_index("tensor")
    acc[...] = dot(gfac[...], left[...], 1, 1)
    for k in range(npan):
        panel = lax.rem(me + k, npan)
        for s in range(slots):

            @pl.when(s < live[panel])
            def _():
                where = pl.ds(pl.multiple_of(pairs[panel, s, 0] * blk, blk), blk)
                acc[:, where] = acc[:, where] + parts[k, s].astype(F32)

    dx[...] = acc[...].astype(BF)


def specs(smem, vmem):
    return [pl.BlockSpec(memory_space=pltpu.SMEM)] * smem + [pl.BlockSpec(memory_space=VM)] * vmem


def call(kernel, smem, outs, scratch, args, mib, flops):
    return pl.pallas_call(
        kernel,
        out_shape=[jax.ShapeDtypeStruct(s, d) for s, d in outs],
        in_specs=specs(smem, len(args) - smem),
        out_specs=specs(0, len(outs)),
        scratch_shapes=[pltpu.VMEM(s, d) for s, d in scratch],
        compiler_params=pltpu.CompilerParams(vmem_limit_bytes=mib << 20),
        cost_estimate=pl.CostEstimate(flops=flops, bytes_accessed=mib << 18, transcendentals=0),
    )(*args)


def shift_over(axis, value, k):
    n = lax.axis_size(axis)
    return lax.ppermute(value, axis, [(i, (i + k) % n) for i in range(n)])


def pick(value, index, axis):
    return lax.dynamic_index_in_dim(value, index, axis, keepdims=False)


def over_cores_and_dp(keep, give):
    summed = keep.astype(F32) + shift_over("seq", give, 1).astype(F32)
    ndp = lax.axis_size("dp")
    d = lax.axis_index("dp")
    total = pick(summed, d, 0)
    for j in range(1, ndp):
        away = pick(summed, lax.rem(d + j, ndp), 0).astype(BF)
        total = total + shift_over("dp", away, j).astype(F32)
    return total


def per_device(tokens, grad_out, up_blocks, down_blocks, pairs, live, left_factor, right_factor):
    npan, ndp, nseq = lax.axis_size("tensor"), lax.axis_size("dp"), lax.axis_size("seq")
    core, grp = lax.axis_index("seq"), lax.axis_index("groups")
    x, dy = tokens[0], grad_out[0]
    toks, width = x.shape
    slots, blk = up_blocks.shape[1], up_blocks.shape[2]
    rank, pwidth = right_factor.shape
    ncols = pwidth // blk
    assert nseq == 2 and slots == 2 and lax.axis_size("groups") == 2 and ncols == 4
    rows = blk // (ndp * nseq)
    rk = rank // (ndp * nseq)

    quarter = jnp.concatenate(
        [
            jnp.where(grp == 0, pick(up_blocks[0], core, 0), pick(down_blocks[0], core, 0)),
            lax.dynamic_slice_in_dim(right_factor, (grp * 2 + core) * blk, blk, 1),
        ],
        axis=0,
    )
    order = [npan // 2] + [k for k in range(1, npan) if k != npan // 2]
    got = {}
    for k in order:
        got[k] = shift_over("tensor", quarter, npan - k)

    grad_shape = (ndp, 2, slots, rows, blk)
    term_outs = [
        (grad_shape, BF),
        (grad_shape, BF),
        ((slots, toks, blk), BF),
        ((toks, rank), F32),
        ((rank, pwidth), F32),
    ]
    flops = 10 * slots * toks * blk * blk
    xg, dyg, factor, keep0, give0, parts0, gacc0, rgrad0 = call(
        functools.partial(own_kernel, ndp, nseq), 2,
        [((npan, slots, toks, blk), BF), ((npan, slots, toks, blk), BF), ((toks, rank), BF)] + term_outs,
        [], (pairs, live, x, dy, left_factor, up_blocks, down_blocks, right_factor), 24, flops,
    )
    parts, gacc, rgrad = {0: parts0}, {0: gacc0}, {0: rgrad0}
    sums = {0: over_cores_and_dp(keep0, give0)}
    for k in order:
        near = jnp.stack([got[k], shift_over("groups", got[k], 1)])
        far = shift_over("seq", near, 1)
        keep, give, parts[k], gacc[k], rgrad[k] = call(
            functools.partial(far_kernel, ndp, nseq, k), 2, term_outs,
            [((2, nseq, blk, blk), BF), ((ncols, rank, blk), BF)],
            (pairs, live, xg[k], dyg[k], factor, near, far), 12, flops,
        )
        sums[k] = over_cores_and_dp(keep, give)

    gfac, lkeep, lgive = call(
        functools.partial(left_kernel, ndp, nseq), 0,
        [((toks, rank), BF)] + [((npan, ndp * rk, width // npan + pwidth), F32)] * 2, [],
        (x, jnp.stack([gacc[k] for k in range(npan)]), jnp.stack([rgrad[k] for k in range(npan)])), 24, 2 * rank * toks * width,
    )
    shape = (npan, ndp, rk, width // npan + pwidth)
    low = over_cores_and_dp(lkeep.reshape(shape).swapaxes(0, 1), lgive.reshape(shape).swapaxes(0, 1))
    (dx,) = call(
        dx_kernel, 2, [((toks, width), BF)], [((toks, width), F32)],
        (pairs, live, left_factor, gfac, jnp.stack([parts[k] for k in range(npan)])), 24, 2 * rank * toks * width,
    )
    total, low_total = sums[0], low[0]
    for k in order:
        total = total + shift_over("tensor", sums[k].astype(BF), k).astype(F32)
        low_total = low_total + shift_over("tensor", low[k].astype(BF), k).astype(F32)
    left = low_total[:, : width // npan].T
    return dx[None], total[0][None], total[1][None], left, low_total[:, width // npan :]


def solution(mesh):
    return jax.shard_map(
        per_device,
        mesh=mesh,
        in_specs=(
            P(("groups", "dp", "seq"), "tensor", None),
            P(("groups", "dp", "seq"), "tensor", None),
            P("tensor", None, None, None),
            P("tensor", None, None, None),
            P(),
            P(),
            P(),
            P(None, "tensor"),
        ),
        out_specs=(
            P(("groups", "dp", "seq"), "tensor", None),
            P(("groups", "tensor"), None, ("dp", "seq"), None),
            P(("groups", "tensor"), None, ("dp", "seq"), None),
            P(("groups", "tensor"), ("dp", "seq")),
            P(("groups", "dp", "seq"), "tensor"),
        ),
        check_vma=False,
    )
```

```python
import functools
import itertools

import jax
import jax.numpy as jnp
from jax import lax
from jax.experimental import pallas as pl
from jax.experimental.pallas import tpu as pltpu
from jax.sharding import PartitionSpec as P

BF = jnp.bfloat16
F32 = jnp.float32
VM, SM, HBM = pltpu.VMEM, pltpu.SMEM, pltpu.HBM
PLANE = ("tensor", "dp", "seq")


def dot(a, b, ca, cb):
    return lax.dot_general(a, b, (((ca,), (cb,)), ((), ())), preferred_element_type=F32)


def class_of(d, c, ndp):
    return c * ndp + (d ^ (c * (ndp - 1)))


def plane(ndp, nseq):
    return [(i, j) for i in range(ndp)[::-1] for j in range(nseq)[::-1]]


def block(ref, index, size, axis=1):
    where = pl.ds(pl.multiple_of(index * size, size), size)
    return ref.at[:, where] if axis == 1 else ref.at[where]


def collect_kernel(dims, pairs, x, dy, left, up, down, right, *refs):
    ndp, nseq, turns = dims
    nclass = ndp * nseq
    weights, outs = refs[0], refs[1 : 1 + nclass]
    xbuf, lbuf, sems = refs[1 + nclass :]
    slots, blk = up.shape[:2]
    toks = x.shape[0]
    rank, ncols = right.shape[0], right.shape[1] // blk
    me, d, c = (lax.axis_index(a) for a in PLANE)
    copies = [pltpu.make_async_copy(left, lbuf, sems.at[0])]
    parts = 4
    rows = toks // parts
    for n in range(parts):
        here = pl.ds(n * rows, rows)
        copies.append(pltpu.make_async_copy(x.at[here], xbuf.at[here], sems.at[1 + n]))
    first = len(copies)
    moves = []
    for a, src in enumerate((up, down)):
        for s in range(slots):
            moves.append((src.at[s], weights.at[pl.ds((a * slots + s) * blk, blk)]))
    for j in range(ncols):
        moves.append((right.at[:, pl.ds(j * blk, blk)], weights.at[pl.ds(2 * slots * blk + j * rank, rank)]))
    for (i, j), out in zip(plane(ndp, nseq), outs):
        cls = class_of(d ^ i, c ^ j, ndp)
        for t in range(turns):
            panel = me ^ (cls + t * nclass)
            for a, src in enumerate((x, dy)):
                for s in range(slots):
                    row = ((t * 2 + a) * slots + s) * toks
                    moves.append((block(src, pairs[s, 0, panel], blk), out.at[pl.ds(row, toks)]))
    for n, (src, dst) in enumerate(moves):
        copies.append(pltpu.make_async_copy(src, dst, sems.at[first + n]))
    for copy in copies:
        copy.start()
    for copy in copies[:first]:
        copy.wait()
    factor = dot(lbuf[...], xbuf[...], 1, 1).astype(BF)
    for out in outs:
        tail = pl.ds(out.shape[0] - rank, rank)
        out[tail] = jnp.zeros((rank, blk), BF)
        out[tail, :toks] = factor
    for copy in copies[first:]:
        copy.wait()


def panel_kernel(dims, turn, pairs, live, weights, *refs):
    ndp, nseq, turns = dims
    nclass = ndp * nseq
    tokens, refs = refs[:nclass], refs[nclass:]
    grads, rgrad = refs[:2]
    parts, gfacs, (xcol, dycol, fact) = refs[2 : 2 + nseq], refs[2 + nseq : 2 + 2 * nseq], refs[2 + 2 * nseq :]
    slots, rows, blk = grads.shape[3:]
    rank = rgrad.shape[0]
    toks = fact.shape[1] // nclass
    me, d, c = (lax.axis_index(a) for a in PLANE)
    panel = me ^ (class_of(d, c, ndp) + turn * nclass)
    for n, src in enumerate(tokens):
        here = slice(n * toks, (n + 1) * toks)
        for s in range(slots):
            for a, dst in ((0, xcol), (1, dycol)):
                row = ((turn * 2 + a) * slots + s) * toks
                dst[s, here] = src[row : row + toks]
        fact[:, here] = src[src.shape[0] - rank :, :toks]
    cols = [pairs[s, 1, panel] for s in range(slots)]
    alive = [s < live[panel] for s in range(slots)]
    up = [weights[s * blk : (s + 1) * blk] for s in range(slots)]
    down = [weights[(slots + s) * blk : (slots + s + 1) * blk] for s in range(slots)]
    right = [weights[pl.ds(pl.multiple_of(2 * slots * blk + c_ * rank, rank), rank)] for c_ in cols]
    block_up = [dot(xcol[s], up[s], 1, 0) for s in range(slots)]
    block_down = [dot(dycol[s], down[s], 1, 1) for s in range(slots)]
    rgrad[...] = jnp.zeros(rgrad.shape, F32)
    gsum = None
    for s in range(slots):
        pre = dot(fact[...], right[s], 0, 0)
        dh = jnp.zeros(pre.shape, F32)
        single = alive[s]
        for t in range(slots):
            same = jnp.logical_and(cols[t] == cols[s], alive[t])
            pre = pre + jnp.where(same, block_up[t], 0.0)
            dh = dh + jnp.where(same, block_down[t], 0.0)
            if t < s:
                single = jnp.logical_and(single, jnp.logical_not(same))
        act = pre.astype(BF).astype(F32)
        sig = jax.nn.sigmoid(act)
        hid = (act * sig).astype(BF)
        dpre = (dh * (sig * (1.0 + act * (1.0 - sig)))).astype(BF)
        once = jnp.where(single, dpre, jnp.zeros_like(dpre))
        term = dot(right[s], once, 1, 1)
        gsum = term if gsum is None else gsum + term
        where = pl.ds(pl.multiple_of(cols[s] * blk, blk), blk)
        rgrad[:, where] = rgrad[:, where] + dot(fact[...], once, 1, 0)
        part = jnp.where(alive[s], dot(dpre, up[s], 1, 1), 0.0).astype(BF)
        for n, (i, j) in enumerate(plane(ndp, nseq)):
            parts[j][i, s * toks : (s + 1) * toks] = part[n * toks : (n + 1) * toks]
        gup = jnp.where(alive[s], dot(xcol[s], dpre, 0, 0), 0.0).astype(BF)
        gdown = jnp.where(alive[s], dot(hid, dycol[s], 0, 0), 0.0).astype(BF)
        for a, grad in ((0, gup), (1, gdown)):
            for i, j in itertools.product(range(ndp), range(nseq)):
                lo = (i * nseq + j) * rows
                grads[i, j, a, s] = grad[lo : lo + rows]
    for n, (i, j) in enumerate(plane(ndp, nseq)):
        gfacs[j][i] = gsum[:, n * toks : (n + 1) * toks]


def split_seq(value, ndp, nseq, here):
    rows = value.shape[0] // (ndp * nseq)
    v = [[value[(d * nseq + s) * rows : (d * nseq + s + 1) * rows] for d in range(ndp)] for s in range(nseq)]
    first, second = jnp.stack(v[0]), jnp.stack(v[1])
    return jnp.where(here == 0, first, second), jnp.where(here == 0, second, first)


def left_kernel(dims, x, total, gfac, keep, give):
    ndp, nseq, turns = dims
    npan, chunk = keep.shape[1], keep.shape[3]
    me, here = lax.axis_index("tensor"), lax.axis_index("seq")
    gf = total[...].astype(BF)
    gfac[...] = gf
    for k in range(npan):
        lg = dot(gf, block(x, me ^ k, chunk)[...], 1, 0)
        mine, other = split_seq(lg, ndp, nseq, here)
        for d in range(ndp):
            keep[d, k] = mine[d]
            give[d, k] = other[d]


def dx_kernel(dims, pairs, live, left, gfac, *refs):
    ndp, nseq, turns = dims
    parts, (dx, acc) = refs[:-2], refs[-2:]
    toks = dx.shape[0]
    blk = parts[0].shape[1]
    slots = parts[0].shape[0] // toks
    me, d, c = (lax.axis_index(a) for a in PLANE)
    acc[...] = dot(gfac[...], left[...], 0, 0)
    places = []
    for t in range(turns):
        per = parts[t * (nseq + ndp - 1) : (t + 1) * (nseq + ndp - 1)]
        places += [(t, 0, j, per[j]) for j in range(nseq)]
        places += [(t, i, j, per[nseq + i - 1].at[j]) for i in range(1, ndp) for j in range(nseq)]
    for t, i, j, part in places:
        panel = me ^ (class_of(d ^ i, c ^ j, ndp) + t * ndp * nseq)
        for s in range(slots):

            @pl.when(s < live[panel])
            def _(s=s, part=part, panel=panel):
                where = pl.ds(pl.multiple_of(pairs[s, 0, panel] * blk, blk), blk)
                acc[:, where] = acc[:, where] + part[s * toks : (s + 1) * toks].astype(F32)

    dx[...] = acc[...].astype(BF)


def call(name, kernel, spaces, outs, scratch, args, mib, flops):
    with jax.named_scope(name):
        return pl.pallas_call(
            kernel,
            out_shape=[jax.ShapeDtypeStruct(s, d) for s, d in outs],
            in_specs=[pl.BlockSpec(memory_space=space) for space in spaces],
            out_specs=[pl.BlockSpec(memory_space=VM)] * len(outs),
            scratch_shapes=scratch,
            compiler_params=pltpu.CompilerParams(vmem_limit_bytes=mib << 20),
            cost_estimate=pl.CostEstimate(flops=flops, bytes_accessed=1024, transcendentals=0),
        )(*args)


def permute(name, value, target):
    sizes = [lax.axis_size(a) for a in PLANE]

    def flat(z, d, c):
        return (z * sizes[1] + d) * sizes[2] + c

    spots = itertools.product(*(range(n) for n in sizes))
    with jax.named_scope(name):
        return lax.ppermute(value, PLANE, [(flat(*spot), flat(*target(*spot))) for spot in spots])


def after(value, *others):
    return lax.optimization_barrier((value, others))[0]


def pick(value, index, axis):
    return lax.dynamic_index_in_dim(value, index, axis, keepdims=False)


def per_device(tokens, grad_out, up_blocks, down_blocks, pairs, live, left_factor, right_factor):
    npan, ndp, nseq = (lax.axis_size(a) for a in PLANE)
    me, dpi, core = (lax.axis_index(a) for a in PLANE)
    x, dy = tokens[0], grad_out[0]
    toks, width = x.shape
    up, down = up_blocks[0], down_blocks[0]
    slots, blk = up.shape[:2]
    rank, pwidth = right_factor.shape
    ncols = pwidth // blk
    nclass = ndp * nseq
    turns = npan // nclass
    assert nseq == 2 and npan == turns * nclass and npan & (npan - 1) == 0 and ndp & (ndp - 1) == 0
    dims = (ndp, nseq, turns)
    rows, rk, chunk = blk // nclass, rank // nclass, width // npan
    pairs, left_t = pairs.transpose(1, 2, 0), left_factor.T
    partners = plane(ndp, nseq)

    def handled(d, c, t):
        return class_of(d, c, ndp) + t * nclass

    wrows = 2 * slots * blk + ncols * rank
    trows = turns * 2 * slots * toks + rank
    ncopy = 5 + 2 * slots + ncols + nclass * turns * 2 * slots
    weights, *sent = call(
        "collect", functools.partial(collect_kernel, dims), [SM] + [HBM] * 6,
        [((wrows, blk), BF)] + [((trows, blk), BF)] * nclass,
        [pltpu.VMEM((toks, width), BF), pltpu.VMEM((rank, width), BF), pltpu.SemaphoreType.DMA((ncopy,))],
        (pairs, *(pltpu.with_memory_space_constraint(v, HBM) for v in (x, dy, left_t, up, down, right_factor))), 16, 10**8,
    )
    held = [permute(f"weights{t}", weights, lambda z, d, c, t=t: (z ^ handled(d, c, t), d, c)) for t in range(turns)]
    got = [
        permute(f"tokens{i}{j}", v, lambda z, d, c, i=i, j=j: (z, d ^ i, c ^ j)) if i or j else v
        for (i, j), v in zip(partners, sent)
    ]
    grads, rights, parts, gfacs = [], [], [], []
    for t in range(turns):
        grad, right, *rest = call(
            f"panel{t}", functools.partial(panel_kernel, dims, t), [SM] * 2 + [VM] * (1 + nclass),
            [((ndp, nseq, 2, slots, rows, blk), BF), ((rank, pwidth), F32)]
            + [((ndp, slots * toks, blk), BF)] * nseq + [((ndp, rank, toks), F32)] * nseq,
            [pltpu.VMEM((slots, nclass * toks, blk), BF)] * 2 + [pltpu.VMEM((rank, nclass * toks), BF)],
            (pairs, live, held[t], *got), 16, 10**8,
        )
        grads.append(grad)
        rights.append(right)
        parts.append(rest[:nseq])
        gfacs.append(rest[nseq:])

    swap = lambda z, d, c: (z, d, c ^ 1)

    def across(name, value, i):
        return permute(f"{name}{i}", value, lambda z, d, c: (z, d ^ i, c))

    own = sum(gfacs[t][0] for t in range(turns))
    own = own + permute("gfac_core", sum(gfacs[t][1] for t in range(turns)), swap)
    gsum = own[0]
    for i in range(1, ndp):
        gsum = gsum + across("gfac_dp", own[i], i)
    gfac, keep, give = call(
        "left", functools.partial(left_kernel, dims), [VM] * 2,
        [((rank, toks), BF)] + [((ndp, npan, rk, chunk), F32)] * 2, [], (x, gsum), 12, 10**8,
    )
    low = keep + permute("left_core", give, swap)
    mine = pick(low, dpi, 0)
    away = [pick(low, dpi ^ i, 0).astype(BF) for i in range(1, ndp)]
    for i in range(1, ndp):
        mine = mine + permute(f"left_dp{i}", away[i - 1], lambda z, d, c, i=i: (z, d ^ i, c)).astype(F32)
    part_all = []
    for t in range(turns):
        near = parts[t][0], permute(f"parts_core{t}", parts[t][1], swap)
        part_all += [v[0] for v in near]
        for i in range(1, ndp):
            leave = after(jnp.stack([v[i] for v in near]), away)
            part_all.append(across(f"parts_dp{t}", leave, i))
    lots = []
    for t in range(turns):
        rsplit = rights[t].reshape(ndp, nseq, rk, pwidth)
        for i in range(ndp):
            lots.append(jnp.concatenate(
                [pick(grads[t], dpi ^ i, 0).reshape(nseq, -1, blk), pick(rsplit, dpi ^ i, 0).astype(BF).reshape(nseq, -1, blk)],
                axis=1,
            ))
    lots = after(lots, away)
    came = [
        permute(f"grads{t}{i}", lots[t * ndp + i], lambda z, d, c, t=t, i=i: (z ^ handled(d, c, t), d ^ i, c))
        for t in range(turns) for i in range(ndp)
    ]
    owned = sum(v.astype(F32) for v in came)
    step = npan
    while step > 1:
        step //= 2
        sent = mine[step:].astype(BF)
        mine = mine[:step] + permute(f"left_tensor{step}", sent, lambda z, d, c, k=step: (z ^ k, d, c)).astype(F32)
    left = mine[0]
    (dx,) = call(
        "dx", functools.partial(dx_kernel, dims), [SM] * 2 + [VM] * (2 + len(part_all)),
        [((toks, width), BF)], [pltpu.VMEM((toks, width), F32)],
        (pairs, live, left_t, gfac, *part_all), 12, 10**8,
    )
    owned = after(owned, dx)
    leave = pick(owned, 1 - core, 0).astype(BF)
    total = pick(owned, core, 0) + permute("grads_core", leave, swap).astype(F32)
    nblock = 2 * slots * rows
    blocks = total[:nblock].reshape(2, 1, slots, rows, blk)
    return dx[None], blocks[0], blocks[1], left.T, total[nblock:].reshape(rk, pwidth)


def solution(mesh):
    return jax.shard_map(
        per_device,
        mesh=mesh,
        in_specs=(
            P(("groups", "dp", "seq"), "tensor", None),
            P(("groups", "dp", "seq"), "tensor", None),
            P("tensor", None, None, None),
            P("tensor", None, None, None),
            P(),
            P(),
            P(),
            P(None, "tensor"),
        ),
        out_specs=(
            P(("groups", "dp", "seq"), "tensor", None),
            P(("groups", "tensor"), None, ("dp", "seq"), None),
            P(("groups", "tensor"), None, ("dp", "seq"), None),
            P(("groups", "tensor"), ("dp", "seq")),
            P(("groups", "dp", "seq"), "tensor"),
        ),
        check_vma=False,
    )
```

```python
import functools
import itertools

import jax
import jax.numpy as jnp
from jax import lax
from jax.experimental import pallas as pl
from jax.experimental.pallas import tpu as pltpu
from jax.sharding import PartitionSpec as P

BF = jnp.bfloat16
F32 = jnp.float32
VM, SM, HBM = pltpu.VMEM, pltpu.SMEM, pltpu.HBM
PLANE = ("tensor", "dp", "seq")


def dot(a, b, ca, cb):
    return lax.dot_general(a, b, (((ca,), (cb,)), ((), ())), preferred_element_type=F32)


def class_of(d, c, ndp):
    return c * ndp + (d ^ (c * (ndp - 1)))


def plane(ndp, nseq):
    return [(i, j) for i in range(ndp)[::-1] for j in range(nseq)[::-1]]


def block(ref, index, size, axis=1):
    where = pl.ds(pl.multiple_of(index * size, size), size)
    return ref.at[:, where] if axis == 1 else ref.at[where]


def collect_kernel(dims, pairs, x, dy, left, up, down, right, *refs):
    ndp, nseq, turns = dims
    nclass = ndp * nseq
    weights, outs = refs[0], refs[1 : 1 + nclass]
    xbuf, lbuf, table, sems = refs[1 + nclass :]
    look = pltpu.make_async_copy(pairs, table, sems.at[sems.shape[0] - 1])
    look.start()
    slots, blk = up.shape[:2]
    toks = x.shape[0]
    rank, ncols = right.shape[0], right.shape[1] // blk
    me, d, c = (lax.axis_index(a) for a in PLANE)
    copies = [pltpu.make_async_copy(left, lbuf, sems.at[0])]
    parts = 4
    rows = toks // parts
    for n in range(parts):
        here = pl.ds(n * rows, rows)
        copies.append(pltpu.make_async_copy(x.at[here], xbuf.at[here], sems.at[1 + n]))
    first = len(copies)
    moves = []
    for a, src in enumerate((up, down)):
        for s in range(slots):
            moves.append((src.at[s], weights.at[pl.ds((a * slots + s) * blk, blk)]))
    for j in range(ncols):
        moves.append((right.at[:, pl.ds(j * blk, blk)], weights.at[pl.ds(2 * slots * blk + j * rank, rank)]))
    for n, (src, dst) in enumerate(moves):
        copies.append(pltpu.make_async_copy(src, dst, sems.at[first + n]))
    for copy in copies:
        copy.start()
    look.wait()
    for (i, j), out in zip(plane(ndp, nseq), outs):
        cls = class_of(d ^ i, c ^ j, ndp)
        for t in range(turns):
            panel = me ^ (cls + t * nclass)
            for s in range(slots):
                row = table[s, 0, panel]
                for a, src in enumerate((x, dy)):
                    lo = ((t * 2 + a) * slots + s) * toks
                    copy = pltpu.make_async_copy(block(src, row, blk), out.at[pl.ds(lo, toks)], sems.at[len(copies)])
                    copy.start()
                    copies.append(copy)
    for copy in copies[:first]:
        copy.wait()
    factor = dot(lbuf[...], xbuf[...], 1, 1).astype(BF)
    for out in outs:
        tail = pl.ds(out.shape[0] - rank, rank)
        out[tail] = jnp.zeros((rank, blk), BF)
        out[tail, :toks] = factor
    for copy in copies[first:]:
        copy.wait()


def panel_kernel(dims, turn, pairs, live, weights, *refs):
    ndp, nseq, turns = dims
    nclass = ndp * nseq
    tokens, refs = refs[:nclass], refs[nclass:]
    grads, rgrad = refs[:2]
    parts, gfacs, (xcol, dycol, fact) = refs[2 : 2 + nseq], refs[2 + nseq : 2 + 2 * nseq], refs[2 + 2 * nseq :]
    slots, rows, blk = grads.shape[3:]
    rank = rgrad.shape[0]
    toks = fact.shape[1] // nclass
    me, d, c = (lax.axis_index(a) for a in PLANE)
    panel = me ^ (class_of(d, c, ndp) + turn * nclass)
    for n, src in enumerate(tokens):
        here = slice(n * toks, (n + 1) * toks)
        for s in range(slots):
            for a, dst in ((0, xcol), (1, dycol)):
                row = ((turn * 2 + a) * slots + s) * toks
                dst[s, here] = src[row : row + toks]
        fact[:, here] = src[src.shape[0] - rank :, :toks]
    cols = [pairs[s, 1, panel] for s in range(slots)]
    alive = [s < live[panel] for s in range(slots)]
    up = [weights[s * blk : (s + 1) * blk] for s in range(slots)]
    down = [weights[(slots + s) * blk : (slots + s + 1) * blk] for s in range(slots)]
    right = [weights[pl.ds(pl.multiple_of(2 * slots * blk + c_ * rank, rank), rank)] for c_ in cols]
    block_up = [dot(xcol[s], up[s], 1, 0) for s in range(slots)]
    block_down = [dot(dycol[s], down[s], 1, 1) for s in range(slots)]
    rgrad[...] = jnp.zeros(rgrad.shape, F32)
    gsum = None
    for s in range(slots):
        pre = dot(fact[...], right[s], 0, 0)
        dh = jnp.zeros(pre.shape, F32)
        single = alive[s]
        for t in range(slots):
            same = jnp.logical_and(cols[t] == cols[s], alive[t])
            pre = pre + jnp.where(same, block_up[t], 0.0)
            dh = dh + jnp.where(same, block_down[t], 0.0)
            if t < s:
                single = jnp.logical_and(single, jnp.logical_not(same))
        act = pre.astype(BF).astype(F32)
        sig = jax.nn.sigmoid(act)
        hid = (act * sig).astype(BF)
        dpre = (dh * (sig * (1.0 + act * (1.0 - sig)))).astype(BF)
        once = jnp.where(single, dpre, jnp.zeros_like(dpre))
        term = dot(right[s], once, 1, 1)
        gsum = term if gsum is None else gsum + term
        where = pl.ds(pl.multiple_of(cols[s] * blk, blk), blk)
        rgrad[:, where] = rgrad[:, where] + dot(fact[...], once, 1, 0)
        part = jnp.where(alive[s], dot(dpre, up[s], 1, 1), 0.0).astype(BF)
        for n, (i, j) in enumerate(plane(ndp, nseq)):
            parts[j][i, s * toks : (s + 1) * toks] = part[n * toks : (n + 1) * toks]
        gup = jnp.where(alive[s], dot(xcol[s], dpre, 0, 0), 0.0).astype(BF)
        gdown = jnp.where(alive[s], dot(hid, dycol[s], 0, 0), 0.0).astype(BF)
        for a, grad in ((0, gup), (1, gdown)):
            for i, j in itertools.product(range(ndp), range(nseq)):
                lo = (i * nseq + j) * rows
                grads[i, j, a, s] = grad[lo : lo + rows]
    for n, (i, j) in enumerate(plane(ndp, nseq)):
        gfacs[j][i] = gsum[:, n * toks : (n + 1) * toks]


def split_seq(value, ndp, nseq, here):
    rows = value.shape[0] // (ndp * nseq)
    v = [[value[(d * nseq + s) * rows : (d * nseq + s + 1) * rows] for d in range(ndp)] for s in range(nseq)]
    first, second = jnp.stack(v[0]), jnp.stack(v[1])
    return jnp.where(here == 0, first, second), jnp.where(here == 0, second, first)


def left_kernel(dims, x, total, gfac, keep, give):
    ndp, nseq, turns = dims
    npan, chunk = keep.shape[1], keep.shape[3]
    me, here = lax.axis_index("tensor"), lax.axis_index("seq")
    gf = total[...].astype(BF)
    gfac[...] = gf
    for k in range(npan):
        lg = dot(gf, block(x, me ^ k, chunk)[...], 1, 0)
        mine, other = split_seq(lg, ndp, nseq, here)
        for d in range(ndp):
            keep[d, k] = mine[d]
            give[d, k] = other[d]


def dx_kernel(dims, pairs, live, left, gfac, *refs):
    ndp, nseq, turns = dims
    parts, (dx, acc) = refs[:-2], refs[-2:]
    toks = dx.shape[0]
    blk = parts[0].shape[1]
    slots = parts[0].shape[0] // toks
    me, d, c = (lax.axis_index(a) for a in PLANE)
    acc[...] = dot(gfac[...], left[...], 0, 0)
    places = []
    for t in range(turns):
        per = parts[t * (nseq + ndp - 1) : (t + 1) * (nseq + ndp - 1)]
        places += [(t, 0, j, per[j]) for j in range(nseq)]
        places += [(t, i, j, per[nseq + i - 1].at[j]) for i in range(1, ndp) for j in range(nseq)]
    for t, i, j, part in places:
        panel = me ^ (class_of(d ^ i, c ^ j, ndp) + t * ndp * nseq)
        for s in range(slots):

            @pl.when(s < live[panel])
            def _(s=s, part=part, panel=panel):
                where = pl.ds(pl.multiple_of(pairs[s, 0, panel] * blk, blk), blk)
                acc[:, where] = acc[:, where] + part[s * toks : (s + 1) * toks].astype(F32)

    dx[...] = acc[...].astype(BF)


def finish_kernel(nblock, mine, other, left, up, down, right, left_out):
    slots, rows, blk = up.shape
    total = mine[...] + other[...].astype(F32)
    for a, out in ((0, up), (1, down)):
        for s in range(slots):
            lo = (a * slots + s) * rows
            out[s] = total[lo : lo + rows]
    width = right.shape[1]
    per = width // blk
    for r in range(right.shape[0]):
        for j in range(per):
            lo = nblock + r * per + j
            right[r : r + 1, j * blk : (j + 1) * blk] = total[lo : lo + 1]
    left_out[...] = left[...]


def call(name, kernel, spaces, outs, scratch, args, mib, flops):
    with jax.named_scope(name):
        return pl.pallas_call(
            kernel,
            out_shape=[jax.ShapeDtypeStruct(s, d) for s, d in outs],
            in_specs=[pl.BlockSpec(memory_space=space) for space in spaces],
            out_specs=[pl.BlockSpec(memory_space=VM)] * len(outs),
            scratch_shapes=scratch,
            compiler_params=pltpu.CompilerParams(vmem_limit_bytes=mib << 20),
            cost_estimate=pl.CostEstimate(flops=flops, bytes_accessed=1024, transcendentals=0),
        )(*args)


def permute(name, value, target):
    sizes = [lax.axis_size(a) for a in PLANE]

    def flat(z, d, c):
        return (z * sizes[1] + d) * sizes[2] + c

    spots = itertools.product(*(range(n) for n in sizes))
    with jax.named_scope(name):
        return lax.ppermute(value, PLANE, [(flat(*spot), flat(*target(*spot))) for spot in spots])


def after(value, *others):
    return lax.optimization_barrier((value, others))[0]


def pick(value, index, axis):
    return lax.dynamic_index_in_dim(value, index, axis, keepdims=False)


def per_device(tokens, grad_out, up_blocks, down_blocks, pairs, live, left_factor, right_factor):
    npan, ndp, nseq = (lax.axis_size(a) for a in PLANE)
    me, dpi, core = (lax.axis_index(a) for a in PLANE)
    x, dy = tokens[0], grad_out[0]
    toks, width = x.shape
    up, down = up_blocks[0], down_blocks[0]
    slots, blk = up.shape[:2]
    rank, pwidth = right_factor.shape
    ncols = pwidth // blk
    nclass = ndp * nseq
    turns = npan // nclass
    assert nseq == 2 and npan == turns * nclass and npan & (npan - 1) == 0 and ndp & (ndp - 1) == 0
    dims = (ndp, nseq, turns)
    rows, rk, chunk = blk // nclass, rank // nclass, width // npan
    pairs, left_t = pairs.transpose(1, 2, 0), left_factor.T
    partners = plane(ndp, nseq)

    def handled(d, c, t):
        return class_of(d, c, ndp) + t * nclass

    wrows = 2 * slots * blk + ncols * rank
    trows = turns * 2 * slots * toks + rank
    ncopy = 5 + 2 * slots + ncols + nclass * turns * 2 * slots
    weights, *sent = call(
        "collect", functools.partial(collect_kernel, dims), [HBM] * 7,
        [((wrows, blk), BF)] + [((trows, blk), BF)] * nclass,
        [pltpu.VMEM((toks, width), BF), pltpu.VMEM((rank, width), BF), pltpu.SMEM(pairs.shape, jnp.int32), pltpu.SemaphoreType.DMA((ncopy + 1,))],
        tuple(pltpu.with_memory_space_constraint(v, HBM) for v in (pairs, x, dy, left_t, up, down, right_factor)), 16, 10**8,
    )
    held = [permute(f"weights{t}", weights, lambda z, d, c, t=t: (z ^ handled(d, c, t), d, c)) for t in range(turns)]
    got = [
        permute(f"tokens{i}{j}", v, lambda z, d, c, i=i, j=j: (z, d ^ i, c ^ j)) if i or j else v
        for (i, j), v in zip(partners, sent)
    ]
    grads, rights, parts, gfacs = [], [], [], []
    for t in range(turns):
        grad, right, *rest = call(
            f"panel{t}", functools.partial(panel_kernel, dims, t), [SM] * 2 + [VM] * (1 + nclass),
            [((ndp, nseq, 2, slots, rows, blk), BF), ((rank, pwidth), F32)]
            + [((ndp, slots * toks, blk), BF)] * nseq + [((ndp, rank, toks), F32)] * nseq,
            [pltpu.VMEM((slots, nclass * toks, blk), BF)] * 2 + [pltpu.VMEM((rank, nclass * toks), BF)],
            (pairs, live, held[t], *got), 16, 10**8,
        )
        grads.append(grad)
        rights.append(right)
        parts.append(rest[:nseq])
        gfacs.append(rest[nseq:])

    swap = lambda z, d, c: (z, d, c ^ 1)

    def across(name, value, i):
        return permute(f"{name}{i}", value, lambda z, d, c: (z, d ^ i, c))

    own = sum(gfacs[t][0] for t in range(turns))
    own = own + permute("gfac_core", sum(gfacs[t][1] for t in range(turns)), swap)
    gsum = own[0]
    for i in range(1, ndp):
        gsum = gsum + across("gfac_dp", own[i], i)
    gfac, keep, give = call(
        "left", functools.partial(left_kernel, dims), [VM] * 2,
        [((rank, toks), BF)] + [((ndp, npan, rk, chunk), F32)] * 2, [], (x, gsum), 12, 10**8,
    )
    low = keep + permute("left_core", give, swap)
    mine = pick(low, dpi, 0)
    away = [pick(low, dpi ^ i, 0).astype(BF) for i in range(1, ndp)]
    for i in range(1, ndp):
        mine = mine + permute(f"left_dp{i}", away[i - 1], lambda z, d, c, i=i: (z, d ^ i, c)).astype(F32)
    part_all = []
    for t in range(turns):
        near = parts[t][0], permute(f"parts_core{t}", parts[t][1], swap)
        part_all += [v[0] for v in near]
        for i in range(1, ndp):
            leave = after(jnp.stack([v[i] for v in near]), away)
            part_all.append(across(f"parts_dp{t}", leave, i))
    lots = []
    for t in range(turns):
        rsplit = rights[t].reshape(ndp, nseq, rk, pwidth)
        for i in range(ndp):
            lots.append(jnp.concatenate(
                [pick(grads[t], dpi ^ i, 0).reshape(nseq, -1, blk), pick(rsplit, dpi ^ i, 0).astype(BF).reshape(nseq, -1, blk)],
                axis=1,
            ))
    lots = after(lots, away)
    came = [
        permute(f"grads{t}{i}", lots[t * ndp + i], lambda z, d, c, t=t, i=i: (z ^ handled(d, c, t), d ^ i, c))
        for t in range(turns) for i in range(ndp)
    ]
    owned = sum(v.astype(F32) for v in came)
    step = npan
    while step > 1:
        step //= 2
        sent = mine[step:].astype(BF)
        mine = mine[:step] + permute(f"left_tensor{step}", sent, lambda z, d, c, k=step: (z ^ k, d, c)).astype(F32)
    left = mine[0]
    (dx,) = call(
        "dx", functools.partial(dx_kernel, dims), [SM] * 2 + [VM] * (2 + len(part_all)),
        [((toks, width), BF)], [pltpu.VMEM((toks, width), F32)],
        (pairs, live, left_t, gfac, *part_all), 12, 10**8,
    )
    owned = after(owned, dx)
    leave = pick(owned, 1 - core, 0).astype(BF)
    swapped = permute("grads_core", leave, swap)
    nblock = 2 * slots * rows
    up_sum, down_sum, right_sum, left_sum = call(
        "finish", functools.partial(finish_kernel, nblock), [VM] * 3,
        [((slots, rows, blk), F32)] * 2 + [((rk, pwidth), F32), ((rk, chunk), F32)], [],
        (pick(owned, core, 0), swapped, left), 4, 10**6,
    )
    return dx[None], up_sum[None], down_sum[None], left_sum.T, right_sum


def solution(mesh):
    return jax.shard_map(
        per_device,
        mesh=mesh,
        in_specs=(
            P(("groups", "dp", "seq"), "tensor", None),
            P(("groups", "dp", "seq"), "tensor", None),
            P("tensor", None, None, None),
            P("tensor", None, None, None),
            P(),
            P(),
            P(),
            P(None, "tensor"),
        ),
        out_specs=(
            P(("groups", "dp", "seq"), "tensor", None),
            P(("groups", "tensor"), None, ("dp", "seq"), None),
            P(("groups", "tensor"), None, ("dp", "seq"), None),
            P(("groups", "tensor"), ("dp", "seq")),
            P(("groups", "dp", "seq"), "tensor"),
        ),
        check_vma=False,
    )
```

```python
import functools
import itertools

import jax
import jax.numpy as jnp
from jax import lax
from jax.experimental import pallas as pl
from jax.experimental.pallas import tpu as pltpu
from jax.sharding import PartitionSpec as P

BF = jnp.bfloat16
F32 = jnp.float32
VM, SM, HBM = pltpu.VMEM, pltpu.SMEM, pltpu.HBM
PLANE = ("tensor", "dp", "seq")


def dot(a, b, ca, cb):
    return lax.dot_general(a, b, (((ca,), (cb,)), ((), ())), preferred_element_type=F32)


def class_of(d, c, ndp):
    return c * ndp + (d ^ (c * (ndp - 1)))


def plane(ndp, nseq):
    return [(i, j) for i in range(ndp)[::-1] for j in range(nseq)[::-1]]


def block(ref, index, size, axis=1):
    where = pl.ds(pl.multiple_of(index * size, size), size)
    return ref.at[:, where] if axis == 1 else ref.at[where]


def collect_kernel(dims, pairs, x, dy, left, up, down, right, *refs):
    ndp, nseq, turns = dims
    nclass = ndp * nseq
    weights, outs = refs[0], refs[1 : 1 + nclass]
    xbuf, lbuf, table, sems = refs[1 + nclass :]
    look = pltpu.make_async_copy(pairs, table, sems.at[sems.shape[0] - 1])
    look.start()
    slots, blk = up.shape[:2]
    toks = x.shape[0]
    rank, ncols = right.shape[0], right.shape[1] // blk
    me, d, c = (lax.axis_index(a) for a in PLANE)
    copies = [pltpu.make_async_copy(left, lbuf, sems.at[0])]
    parts = 4
    rows = toks // parts
    for n in range(parts):
        here = pl.ds(n * rows, rows)
        copies.append(pltpu.make_async_copy(x.at[here], xbuf.at[here], sems.at[1 + n]))
    first = len(copies)
    moves = []
    for a, src in enumerate((up, down)):
        for s in range(slots):
            moves.append((src.at[s], weights.at[pl.ds((a * slots + s) * blk, blk)]))
    for j in range(ncols):
        moves.append((right.at[:, pl.ds(j * blk, blk)], weights.at[pl.ds(2 * slots * blk + j * rank, rank)]))
    for n, (src, dst) in enumerate(moves):
        copies.append(pltpu.make_async_copy(src, dst, sems.at[first + n]))
    for copy in copies:
        copy.start()
    look.wait()
    for (i, j), out in zip(plane(ndp, nseq), outs):
        cls = class_of(d ^ i, c ^ j, ndp)
        for t in range(turns):
            panel = me ^ (cls + t * nclass)
            for s in range(slots):
                row = table[s, 0, panel]
                for a, src in enumerate((x, dy)):
                    lo = ((t * 2 + a) * slots + s) * toks
                    copy = pltpu.make_async_copy(block(src, row, blk), out.at[pl.ds(lo, toks)], sems.at[len(copies)])
                    copy.start()
                    copies.append(copy)
    for copy in copies[:first]:
        copy.wait()
    factor = dot(lbuf[...], xbuf[...], 1, 1).astype(BF)
    for out in outs:
        tail = pl.ds(out.shape[0] - rank, rank)
        out[tail] = jnp.zeros((rank, blk), BF)
        out[tail, :toks] = factor
    for copy in copies[first:]:
        copy.wait()


def panel_kernel(dims, turn, pairs, live, weights, *refs):
    ndp, nseq, turns = dims
    nclass = ndp * nseq
    tokens, refs = refs[:nclass], refs[nclass:]
    xcol, dycol, fact, hidden, dhidden = refs[:5]
    parts, gfacs = refs[5 : 5 + nseq], refs[5 + nseq :]
    slots, _, blk = xcol.shape
    rank = fact.shape[0]
    toks = fact.shape[1] // nclass
    me, d, c = (lax.axis_index(a) for a in PLANE)
    panel = me ^ (class_of(d, c, ndp) + turn * nclass)
    for n, src in enumerate(tokens):
        here = slice(n * toks, (n + 1) * toks)
        for s in range(slots):
            for a, dst in ((0, xcol), (1, dycol)):
                row = ((turn * 2 + a) * slots + s) * toks
                dst[s, here] = src[row : row + toks]
        fact[:, here] = src[src.shape[0] - rank :, :toks]
    cols = [pairs[s, 1, panel] for s in range(slots)]
    alive = [s < live[panel] for s in range(slots)]
    up = [weights[s * blk : (s + 1) * blk] for s in range(slots)]
    down = [weights[(slots + s) * blk : (slots + s + 1) * blk] for s in range(slots)]
    right = [weights[pl.ds(pl.multiple_of(2 * slots * blk + c_ * rank, rank), rank)] for c_ in cols]
    block_up = [dot(xcol[s], up[s], 1, 0) for s in range(slots)]
    block_down = [dot(dycol[s], down[s], 1, 1) for s in range(slots)]
    gsum = None
    for s in range(slots):
        pre = dot(fact[...], right[s], 0, 0)
        dh = jnp.zeros(pre.shape, F32)
        single = alive[s]
        for t in range(slots):
            same = jnp.logical_and(cols[t] == cols[s], alive[t])
            pre = pre + jnp.where(same, block_up[t], 0.0)
            dh = dh + jnp.where(same, block_down[t], 0.0)
            if t < s:
                single = jnp.logical_and(single, jnp.logical_not(same))
        act = pre.astype(BF).astype(F32)
        sig = jax.nn.sigmoid(act)
        hidden[s] = (act * sig).astype(BF)
        dpre = (dh * (sig * (1.0 + act * (1.0 - sig)))).astype(BF)
        dhidden[s] = dpre
        term = jnp.where(single, dot(right[s], dpre, 1, 1), 0.0)
        gsum = term if gsum is None else gsum + term
        part = jnp.where(alive[s], dot(dpre, up[s], 1, 1), 0.0).astype(BF)
        for n, (i, j) in enumerate(plane(ndp, nseq)):
            parts[j][i, s * toks : (s + 1) * toks] = part[n * toks : (n + 1) * toks]
    for n, (i, j) in enumerate(plane(ndp, nseq)):
        gfacs[j][i] = gsum[:, n * toks : (n + 1) * toks]


def grads_kernel(dims, turn, pairs, live, xcol, dycol, fact, hidden, dhidden, grads, rgrad):
    ndp, nseq, turns = dims
    slots, rows, blk = grads.shape[3:]
    me, d, c = (lax.axis_index(a) for a in PLANE)
    panel = me ^ (class_of(d, c, ndp) + turn * ndp * nseq)
    cols = [pairs[s, 1, panel] for s in range(slots)]
    alive = [s < live[panel] for s in range(slots)]
    rgrad[...] = jnp.zeros(rgrad.shape, F32)
    for s in range(slots):
        single = alive[s]
        for t in range(s):
            single = jnp.logical_and(single, jnp.logical_not(jnp.logical_and(cols[t] == cols[s], alive[t])))
        where = pl.ds(pl.multiple_of(cols[s] * blk, blk), blk)
        rgrad[:, where] = rgrad[:, where] + jnp.where(single, dot(fact[...], dhidden[s], 1, 0), 0.0)
        gup = jnp.where(alive[s], dot(xcol[s], dhidden[s], 0, 0), 0.0).astype(BF)
        gdown = jnp.where(alive[s], dot(hidden[s], dycol[s], 0, 0), 0.0).astype(BF)
        for a, grad in ((0, gup), (1, gdown)):
            for i, j in itertools.product(range(ndp), range(nseq)):
                lo = (i * nseq + j) * rows
                grads[i, j, a, s] = grad[lo : lo + rows]


def split_seq(value, ndp, nseq, here):
    rows = value.shape[0] // (ndp * nseq)
    v = [[value[(d * nseq + s) * rows : (d * nseq + s + 1) * rows] for d in range(ndp)] for s in range(nseq)]
    first, second = jnp.stack(v[0]), jnp.stack(v[1])
    return jnp.where(here == 0, first, second), jnp.where(here == 0, second, first)


def left_kernel(dims, x, total, gfac, keep, give):
    ndp, nseq, turns = dims
    npan, chunk = keep.shape[1], keep.shape[3]
    me, here = lax.axis_index("tensor"), lax.axis_index("seq")
    gf = total[...].astype(BF)
    gfac[...] = gf
    for k in range(npan):
        lg = dot(gf, block(x, me ^ k, chunk)[...], 1, 0)
        mine, other = split_seq(lg, ndp, nseq, here)
        for d in range(ndp):
            keep[d, k] = mine[d]
            give[d, k] = other[d]


def dx_kernel(dims, pairs, live, left, gfac, *refs):
    ndp, nseq, turns = dims
    parts, (dx, acc) = refs[:-2], refs[-2:]
    toks = dx.shape[0]
    blk = parts[0].shape[1]
    slots = parts[0].shape[0] // toks
    me, d, c = (lax.axis_index(a) for a in PLANE)
    acc[...] = dot(gfac[...], left[...], 0, 0)
    places = []
    for t in range(turns):
        per = parts[t * (nseq + ndp - 1) : (t + 1) * (nseq + ndp - 1)]
        places += [(t, 0, j, per[j]) for j in range(nseq)]
        places += [(t, i, j, per[nseq + i - 1].at[j]) for i in range(1, ndp) for j in range(nseq)]
    for t, i, j, part in places:
        panel = me ^ (class_of(d ^ i, c ^ j, ndp) + t * ndp * nseq)
        for s in range(slots):

            @pl.when(s < live[panel])
            def _(s=s, part=part, panel=panel):
                where = pl.ds(pl.multiple_of(pairs[s, 0, panel] * blk, blk), blk)
                acc[:, where] = acc[:, where] + part[s * toks : (s + 1) * toks].astype(F32)

    dx[...] = acc[...].astype(BF)


def finish_kernel(nblock, mine, other, left, up, down, right, left_out):
    slots, rows, blk = up.shape
    total = mine[...] + other[...].astype(F32)
    for a, out in ((0, up), (1, down)):
        for s in range(slots):
            lo = (a * slots + s) * rows
            out[s] = total[lo : lo + rows]
    width = right.shape[1]
    per = width // blk
    for r in range(right.shape[0]):
        for j in range(per):
            lo = nblock + r * per + j
            right[r : r + 1, j * blk : (j + 1) * blk] = total[lo : lo + 1]
    left_out[...] = left[...]


def call(name, kernel, spaces, outs, scratch, args, mib, flops):
    with jax.named_scope(name):
        return pl.pallas_call(
            kernel,
            out_shape=[jax.ShapeDtypeStruct(s, d) for s, d in outs],
            in_specs=[pl.BlockSpec(memory_space=space) for space in spaces],
            out_specs=[pl.BlockSpec(memory_space=VM)] * len(outs),
            scratch_shapes=scratch,
            compiler_params=pltpu.CompilerParams(vmem_limit_bytes=mib << 20),
            cost_estimate=pl.CostEstimate(flops=flops, bytes_accessed=1024, transcendentals=0),
        )(*args)


def permute(name, value, target):
    sizes = [lax.axis_size(a) for a in PLANE]

    def flat(z, d, c):
        return (z * sizes[1] + d) * sizes[2] + c

    spots = itertools.product(*(range(n) for n in sizes))
    with jax.named_scope(name):
        return lax.ppermute(value, PLANE, [(flat(*spot), flat(*target(*spot))) for spot in spots])


def after(value, *others):
    return lax.optimization_barrier((value, others))[0]


def pick(value, index, axis):
    return lax.dynamic_index_in_dim(value, index, axis, keepdims=False)


def per_device(tokens, grad_out, up_blocks, down_blocks, pairs, live, left_factor, right_factor):
    npan, ndp, nseq = (lax.axis_size(a) for a in PLANE)
    me, dpi, core = (lax.axis_index(a) for a in PLANE)
    x, dy = tokens[0], grad_out[0]
    toks, width = x.shape
    up, down = up_blocks[0], down_blocks[0]
    slots, blk = up.shape[:2]
    rank, pwidth = right_factor.shape
    ncols = pwidth // blk
    nclass = ndp * nseq
    turns = npan // nclass
    assert nseq == 2 and npan == turns * nclass and npan & (npan - 1) == 0 and ndp & (ndp - 1) == 0
    dims = (ndp, nseq, turns)
    rows, rk, chunk = blk // nclass, rank // nclass, width // npan
    pairs, left_t = pairs.transpose(1, 2, 0), left_factor.T
    partners = plane(ndp, nseq)

    def handled(d, c, t):
        return class_of(d, c, ndp) + t * nclass

    wrows = 2 * slots * blk + ncols * rank
    trows = turns * 2 * slots * toks + rank
    ncopy = 5 + 2 * slots + ncols + nclass * turns * 2 * slots
    weights, *sent = call(
        "collect", functools.partial(collect_kernel, dims), [HBM] * 7,
        [((wrows, blk), BF)] + [((trows, blk), BF)] * nclass,
        [pltpu.VMEM((toks, width), BF), pltpu.VMEM((rank, width), BF), pltpu.SMEM(pairs.shape, jnp.int32), pltpu.SemaphoreType.DMA((ncopy + 1,))],
        tuple(pltpu.with_memory_space_constraint(v, HBM) for v in (pairs, x, dy, left_t, up, down, right_factor)), 16, 10**8,
    )
    held = [permute(f"weights{t}", weights, lambda z, d, c, t=t: (z ^ handled(d, c, t), d, c)) for t in range(turns)]
    got = [
        permute(f"tokens{i}{j}", v, lambda z, d, c, i=i, j=j: (z, d ^ i, c ^ j)) if i or j else v
        for (i, j), v in zip(partners, sent)
    ]
    grads, rights, parts, gfacs = [], [], [], []
    for t in range(turns):
        states = [((slots, nclass * toks, blk), BF)] * 2 + [((rank, nclass * toks), BF)] + [((slots, nclass * toks, blk), BF)] * 2
        *state, p0, p1, g0, g1 = call(
            f"panel{t}", functools.partial(panel_kernel, dims, t), [SM] * 2 + [VM] * (1 + nclass),
            states + [((ndp, slots * toks, blk), BF)] * nseq + [((ndp, rank, toks), F32)] * nseq, [],
            (pairs, live, held[t], *got), 16, 10**8,
        )
        grad, right = call(
            f"grads{t}", functools.partial(grads_kernel, dims, t), [SM] * 2 + [VM] * 5,
            [((ndp, nseq, 2, slots, rows, blk), BF), ((rank, pwidth), F32)], [], (pairs, live, *state), 16, 10**8,
        )
        grads.append(grad)
        rights.append(right)
        parts.append((p0, p1))
        gfacs.append((g0, g1))

    swap = lambda z, d, c: (z, d, c ^ 1)

    def across(name, value, i):
        return permute(f"{name}{i}", value, lambda z, d, c: (z, d ^ i, c))

    own = sum(gfacs[t][0] for t in range(turns))
    own = own + permute("gfac_core", sum(gfacs[t][1] for t in range(turns)), swap)
    gsum = own[0]
    for i in range(1, ndp):
        gsum = gsum + across("gfac_dp", own[i], i)
    gfac, keep, give = call(
        "left", functools.partial(left_kernel, dims), [VM] * 2,
        [((rank, toks), BF)] + [((ndp, npan, rk, chunk), F32)] * 2, [], (x, gsum), 12, 10**8,
    )
    low = keep + permute("left_core", give, swap)
    mine = pick(low, dpi, 0)
    away = [pick(low, dpi ^ i, 0).astype(BF) for i in range(1, ndp)]
    for i in range(1, ndp):
        mine = mine + permute(f"left_dp{i}", away[i - 1], lambda z, d, c, i=i: (z, d ^ i, c)).astype(F32)
    part_all = []
    for t in range(turns):
        near = parts[t][0], permute(f"parts_core{t}", parts[t][1], swap)
        part_all += [v[0] for v in near]
        for i in range(1, ndp):
            leave = after(jnp.stack([v[i] for v in near]), away)
            part_all.append(across(f"parts_dp{t}", leave, i))
    lots = []
    for t in range(turns):
        rsplit = rights[t].reshape(ndp, nseq, rk, pwidth)
        for i in range(ndp):
            lots.append(jnp.concatenate(
                [pick(grads[t], dpi ^ i, 0).reshape(nseq, -1, blk), pick(rsplit, dpi ^ i, 0).astype(BF).reshape(nseq, -1, blk)],
                axis=1,
            ))
    lots = after(lots, away)
    came = [
        permute(f"grads{t}{i}", lots[t * ndp + i], lambda z, d, c, t=t, i=i: (z ^ handled(d, c, t), d ^ i, c))
        for t in range(turns) for i in range(ndp)
    ]
    owned = sum(v.astype(F32) for v in came)
    step = npan
    while step > 1:
        step //= 2
        sent = mine[step:].astype(BF)
        mine = mine[:step] + permute(f"left_tensor{step}", sent, lambda z, d, c, k=step: (z ^ k, d, c)).astype(F32)
    left = mine[0]
    (dx,) = call(
        "dx", functools.partial(dx_kernel, dims), [SM] * 2 + [VM] * (2 + len(part_all)),
        [((toks, width), BF)], [pltpu.VMEM((toks, width), F32)],
        (pairs, live, left_t, gfac, *part_all), 12, 10**8,
    )
    owned = after(owned, dx)
    leave = pick(owned, 1 - core, 0).astype(BF)
    swapped = permute("grads_core", leave, swap)
    nblock = 2 * slots * rows
    up_sum, down_sum, right_sum, left_sum = call(
        "finish", functools.partial(finish_kernel, nblock), [VM] * 3,
        [((slots, rows, blk), F32)] * 2 + [((rk, pwidth), F32), ((rk, chunk), F32)], [],
        (pick(owned, core, 0), swapped, left), 4, 10**6,
    )
    return dx[None], up_sum[None], down_sum[None], left_sum.T, right_sum


def solution(mesh):
    return jax.shard_map(
        per_device,
        mesh=mesh,
        in_specs=(
            P(("groups", "dp", "seq"), "tensor", None),
            P(("groups", "dp", "seq"), "tensor", None),
            P("tensor", None, None, None),
            P("tensor", None, None, None),
            P(),
            P(),
            P(),
            P(None, "tensor"),
        ),
        out_specs=(
            P(("groups", "dp", "seq"), "tensor", None),
            P(("groups", "tensor"), None, ("dp", "seq"), None),
            P(("groups", "tensor"), None, ("dp", "seq"), None),
            P(("groups", "tensor"), ("dp", "seq")),
            P(("groups", "dp", "seq"), "tensor"),
        ),
        check_vma=False,
    )
```

```python
import functools
import itertools

import jax
import jax.numpy as jnp
from jax import lax
from jax.experimental import pallas as pl
from jax.experimental.pallas import tpu as pltpu
from jax.sharding import PartitionSpec as P

BF = jnp.bfloat16
F32 = jnp.float32
VM, SM, HBM = pltpu.VMEM, pltpu.SMEM, pltpu.HBM
PLANE = ("tensor", "dp", "seq")


def dot(a, b, ca, cb):
    return lax.dot_general(a, b, (((ca,), (cb,)), ((), ())), preferred_element_type=F32)


def class_of(d, c, ndp):
    return c * ndp + (d ^ (c * (ndp - 1)))


def plane(ndp, nseq):
    return [(i, j) for i in range(ndp)[::-1] for j in range(nseq)[::-1]]


def block(ref, index, size, axis=1):
    where = pl.ds(pl.multiple_of(index * size, size), size)
    return ref.at[:, where] if axis == 1 else ref.at[where]


def collect_kernel(dims, pairs, x, dy, left, up, down, right, *refs):
    ndp, nseq, turns = dims
    nclass = ndp * nseq
    weights, outs = refs[0], refs[1 : 1 + nclass]
    xbuf, lbuf, table, sems = refs[1 + nclass :]
    look = pltpu.make_async_copy(pairs, table, sems.at[sems.shape[0] - 1])
    look.start()
    slots, blk = up.shape[:2]
    toks = x.shape[0]
    rank, ncols = right.shape[0], right.shape[1] // blk
    me, d, c = (lax.axis_index(a) for a in PLANE)
    copies = [pltpu.make_async_copy(left, lbuf, sems.at[0])]
    parts = 4
    rows = toks // parts
    for n in range(parts):
        here = pl.ds(n * rows, rows)
        copies.append(pltpu.make_async_copy(x.at[here], xbuf.at[here], sems.at[1 + n]))
    first = len(copies)
    moves = []
    for a, src in enumerate((up, down)):
        for s in range(slots):
            moves.append((src.at[s], weights.at[pl.ds((a * slots + s) * blk, blk)]))
    for j in range(ncols):
        moves.append((right.at[:, pl.ds(j * blk, blk)], weights.at[pl.ds(2 * slots * blk + j * rank, rank)]))
    for n, (src, dst) in enumerate(moves):
        copies.append(pltpu.make_async_copy(src, dst, sems.at[first + n]))
    for copy in copies:
        copy.start()
    look.wait()
    for (i, j), out in zip(plane(ndp, nseq), outs):
        cls = class_of(d ^ i, c ^ j, ndp)
        for t in range(turns):
            panel = me ^ (cls + t * nclass)
            for s in range(slots):
                row = table[s, 0, panel]
                lo = ((t * 2 + 1) * slots + s) * toks
                copy = pltpu.make_async_copy(block(dy, row, blk), out.at[pl.ds(lo, toks)], sems.at[len(copies)])
                copy.start()
                copies.append(copy)
    for copy in copies[:first]:
        copy.wait()
    for (i, j), out in zip(plane(ndp, nseq), outs):
        for t in range(turns):
            panel = me ^ (class_of(d ^ i, c ^ j, ndp) + t * nclass)
            for s in range(slots):
                lo = t * 2 * slots * toks + s * toks
                out[lo : lo + toks] = block(xbuf, table[s, 0, panel], blk)[...]
    factor = dot(lbuf[...], xbuf[...], 1, 1).astype(BF)
    for out in outs:
        tail = pl.ds(out.shape[0] - rank, rank)
        out[tail] = jnp.zeros((rank, blk), BF)
        out[tail, :toks] = factor
    for copy in copies[first:]:
        copy.wait()


def panel_kernel(dims, turn, pairs, live, weights, *refs):
    ndp, nseq, turns = dims
    nclass = ndp * nseq
    tokens, refs = refs[:nclass], refs[nclass:]
    xcol, dycol, fact, hidden, dhidden = refs[:5]
    parts, gfacs = refs[5 : 5 + nseq], refs[5 + nseq :]
    slots, _, blk = xcol.shape
    rank = fact.shape[0]
    toks = fact.shape[1] // nclass
    me, d, c = (lax.axis_index(a) for a in PLANE)
    panel = me ^ (class_of(d, c, ndp) + turn * nclass)
    for n, src in enumerate(tokens):
        here = slice(n * toks, (n + 1) * toks)
        for s in range(slots):
            for a, dst in ((0, xcol), (1, dycol)):
                row = ((turn * 2 + a) * slots + s) * toks
                dst[s, here] = src[row : row + toks]
        fact[:, here] = src[src.shape[0] - rank :, :toks]
    cols = [pairs[s, 1, panel] for s in range(slots)]
    alive = [s < live[panel] for s in range(slots)]
    up = [weights[s * blk : (s + 1) * blk] for s in range(slots)]
    down = [weights[(slots + s) * blk : (slots + s + 1) * blk] for s in range(slots)]
    right = [weights[pl.ds(pl.multiple_of(2 * slots * blk + c_ * rank, rank), rank)] for c_ in cols]
    block_up = [dot(xcol[s], up[s], 1, 0) for s in range(slots)]
    block_down = [dot(dycol[s], down[s], 1, 1) for s in range(slots)]
    gsum = None
    for s in range(slots):
        pre = dot(fact[...], right[s], 0, 0)
        dh = 0.0
        single = alive[s]
        for t in range(slots):
            same = jnp.logical_and(cols[t] == cols[s], alive[t])
            if t == s:
                pre, dh = pre + block_up[t], dh + block_down[t]
            else:
                pre = pre + jnp.where(same, block_up[t], 0.0)
                dh = dh + jnp.where(same, block_down[t], 0.0)
            if t < s:
                single = jnp.logical_and(single, jnp.logical_not(same))
        act = pre.astype(BF).astype(F32)
        sig = jax.nn.sigmoid(act)
        hidden[s] = (act * sig).astype(BF)
        dpre = (dh * (sig * (1.0 + act * (1.0 - sig)))).astype(BF)
        dhidden[s] = dpre
        term = jnp.where(single, dot(right[s], dpre, 1, 1), 0.0)
        gsum = term if gsum is None else gsum + term
        part = jnp.where(alive[s], dot(dpre, up[s], 1, 1), 0.0).astype(BF)
        for n, (i, j) in enumerate(plane(ndp, nseq)):
            parts[j][i, s * toks : (s + 1) * toks] = part[n * toks : (n + 1) * toks]
    for n, (i, j) in enumerate(plane(ndp, nseq)):
        gfacs[j][i] = gsum[:, n * toks : (n + 1) * toks]


def grads_kernel(dims, turn, pairs, live, xcol, dycol, fact, hidden, dhidden, grads, rgrad):
    ndp, nseq, turns = dims
    slots, rows, blk = grads.shape[3:]
    me, d, c = (lax.axis_index(a) for a in PLANE)
    panel = me ^ (class_of(d, c, ndp) + turn * ndp * nseq)
    cols = [pairs[s, 1, panel] for s in range(slots)]
    alive = [s < live[panel] for s in range(slots)]
    rgrad[...] = jnp.zeros(rgrad.shape, F32)
    for s in range(slots):
        single = alive[s]
        for t in range(s):
            single = jnp.logical_and(single, jnp.logical_not(jnp.logical_and(cols[t] == cols[s], alive[t])))
        where = pl.ds(pl.multiple_of(cols[s] * blk, blk), blk)
        rgrad[:, where] = rgrad[:, where] + jnp.where(single, dot(fact[...], dhidden[s], 1, 0), 0.0)
        gup = jnp.where(alive[s], dot(xcol[s], dhidden[s], 0, 0), 0.0).astype(BF)
        gdown = jnp.where(alive[s], dot(hidden[s], dycol[s], 0, 0), 0.0).astype(BF)
        for a, grad in ((0, gup), (1, gdown)):
            for i, j in itertools.product(range(ndp), range(nseq)):
                lo = (i * nseq + j) * rows
                grads[i, j, a, s] = grad[lo : lo + rows]


def split_seq(value, ndp, nseq, here):
    rows = value.shape[0] // (ndp * nseq)
    v = [[value[(d * nseq + s) * rows : (d * nseq + s + 1) * rows] for d in range(ndp)] for s in range(nseq)]
    first, second = jnp.stack(v[0]), jnp.stack(v[1])
    return jnp.where(here == 0, first, second), jnp.where(here == 0, second, first)


def left_kernel(dims, x, total, gfac, keep, give):
    ndp, nseq, turns = dims
    npan, chunk = keep.shape[1], keep.shape[3]
    me, here = lax.axis_index("tensor"), lax.axis_index("seq")
    gf = total[...].astype(BF)
    gfac[...] = gf
    for k in range(npan):
        lg = dot(gf, block(x, me ^ k, chunk)[...], 1, 0)
        mine, other = split_seq(lg, ndp, nseq, here)
        for d in range(ndp):
            keep[d, k] = mine[d]
            give[d, k] = other[d]


def dx_kernel(dims, pairs, live, left, gfac, *refs):
    ndp, nseq, turns = dims
    parts, (dx, acc) = refs[:-2], refs[-2:]
    toks = dx.shape[0]
    blk = parts[0].shape[1]
    slots = parts[0].shape[0] // toks
    me, d, c = (lax.axis_index(a) for a in PLANE)
    acc[...] = dot(gfac[...], left[...], 0, 0)
    places = []
    for t in range(turns):
        per = parts[t * (nseq + ndp - 1) : (t + 1) * (nseq + ndp - 1)]
        places += [(t, 0, j, per[j]) for j in range(nseq)]
        places += [(t, i, j, per[nseq + i - 1].at[j]) for i in range(1, ndp) for j in range(nseq)]
    for t, i, j, part in places:
        panel = me ^ (class_of(d ^ i, c ^ j, ndp) + t * ndp * nseq)
        for s in range(slots):

            @pl.when(s < live[panel])
            def _(s=s, part=part, panel=panel):
                where = pl.ds(pl.multiple_of(pairs[s, 0, panel] * blk, blk), blk)
                acc[:, where] = acc[:, where] + part[s * toks : (s + 1) * toks].astype(F32)

    dx[...] = acc[...].astype(BF)


def finish_kernel(nblock, mine, other, left, up, down, right, left_out):
    slots, rows, blk = up.shape
    total = mine[...] + other[...].astype(F32)
    for a, out in ((0, up), (1, down)):
        for s in range(slots):
            lo = (a * slots + s) * rows
            out[s] = total[lo : lo + rows]
    width = right.shape[1]
    per = width // blk
    for r in range(right.shape[0]):
        for j in range(per):
            lo = nblock + r * per + j
            right[r : r + 1, j * blk : (j + 1) * blk] = total[lo : lo + 1]
    left_out[...] = left[...]


def call(name, kernel, spaces, outs, scratch, args, mib, flops):
    with jax.named_scope(name):
        return pl.pallas_call(
            kernel,
            out_shape=[jax.ShapeDtypeStruct(s, d) for s, d in outs],
            in_specs=[pl.BlockSpec(memory_space=space) for space in spaces],
            out_specs=[pl.BlockSpec(memory_space=VM)] * len(outs),
            scratch_shapes=scratch,
            compiler_params=pltpu.CompilerParams(vmem_limit_bytes=mib << 20),
            cost_estimate=pl.CostEstimate(flops=flops, bytes_accessed=1024, transcendentals=0),
        )(*args)


def permute(name, value, target):
    sizes = [lax.axis_size(a) for a in PLANE]

    def flat(z, d, c):
        return (z * sizes[1] + d) * sizes[2] + c

    spots = itertools.product(*(range(n) for n in sizes))
    with jax.named_scope(name):
        return lax.ppermute(value, PLANE, [(flat(*spot), flat(*target(*spot))) for spot in spots])


def after(value, *others):
    return lax.optimization_barrier((value, others))[0]


def pick(value, index, axis):
    return lax.dynamic_index_in_dim(value, index, axis, keepdims=False)


def per_device(tokens, grad_out, up_blocks, down_blocks, pairs, live, left_factor, right_factor):
    npan, ndp, nseq = (lax.axis_size(a) for a in PLANE)
    me, dpi, core = (lax.axis_index(a) for a in PLANE)
    x, dy = tokens[0], grad_out[0]
    toks, width = x.shape
    up, down = up_blocks[0], down_blocks[0]
    slots, blk = up.shape[:2]
    rank, pwidth = right_factor.shape
    ncols = pwidth // blk
    nclass = ndp * nseq
    turns = npan // nclass
    assert nseq == 2 and npan == turns * nclass and npan & (npan - 1) == 0 and ndp & (ndp - 1) == 0
    dims = (ndp, nseq, turns)
    rows, rk, chunk = blk // nclass, rank // nclass, width // npan
    pairs, left_t = pairs.transpose(1, 2, 0), left_factor.T
    partners = plane(ndp, nseq)

    def handled(d, c, t):
        return class_of(d, c, ndp) + t * nclass

    wrows = 2 * slots * blk + ncols * rank
    trows = turns * 2 * slots * toks + rank
    ncopy = 5 + 2 * slots + ncols + nclass * turns * 2 * slots
    weights, *sent = call(
        "collect", functools.partial(collect_kernel, dims), [HBM] * 7,
        [((wrows, blk), BF)] + [((trows, blk), BF)] * nclass,
        [pltpu.VMEM((toks, width), BF), pltpu.VMEM((rank, width), BF), pltpu.SMEM(pairs.shape, jnp.int32), pltpu.SemaphoreType.DMA((ncopy + 1,))],
        tuple(pltpu.with_memory_space_constraint(v, HBM) for v in (pairs, x, dy, left_t, up, down, right_factor)), 16, 10**8,
    )
    held = [permute(f"weights{t}", weights, lambda z, d, c, t=t: (z ^ handled(d, c, t), d, c)) for t in range(turns)]
    got = [
        permute(f"tokens{i}{j}", v, lambda z, d, c, i=i, j=j: (z, d ^ i, c ^ j)) if i or j else v
        for (i, j), v in zip(partners, sent)
    ]
    grads, rights, parts, gfacs = [], [], [], []
    for t in range(turns):
        states = [((slots, nclass * toks, blk), BF)] * 2 + [((rank, nclass * toks), BF)] + [((slots, nclass * toks, blk), BF)] * 2
        *state, p0, p1, g0, g1 = call(
            f"panel{t}", functools.partial(panel_kernel, dims, t), [SM] * 2 + [VM] * (1 + nclass),
            states + [((ndp, slots * toks, blk), BF)] * nseq + [((ndp, rank, toks), F32)] * nseq, [],
            (pairs, live, held[t], *got), 16, 10**8,
        )
        grad, right = call(
            f"grads{t}", functools.partial(grads_kernel, dims, t), [SM] * 2 + [VM] * 5,
            [((ndp, nseq, 2, slots, rows, blk), BF), ((rank, pwidth), F32)], [], (pairs, live, *state), 16, 10**8,
        )
        grads.append(grad)
        rights.append(right)
        parts.append((p0, p1))
        gfacs.append((g0, g1))

    swap = lambda z, d, c: (z, d, c ^ 1)

    def across(name, value, i):
        return permute(f"{name}{i}", value, lambda z, d, c: (z, d ^ i, c))

    own = sum(gfacs[t][0] for t in range(turns))
    own = own + permute("gfac_core", sum(gfacs[t][1] for t in range(turns)), swap)
    gsum = own[0]
    for i in range(1, ndp):
        gsum = gsum + across("gfac_dp", own[i], i)
    gfac, keep, give = call(
        "left", functools.partial(left_kernel, dims), [VM] * 2,
        [((rank, toks), BF)] + [((ndp, npan, rk, chunk), F32)] * 2, [], (x, gsum), 12, 10**8,
    )
    low = keep + permute("left_core", give, swap)
    mine = pick(low, dpi, 0)
    away = [pick(low, dpi ^ i, 0).astype(BF) for i in range(1, ndp)]
    for i in range(1, ndp):
        mine = mine + permute(f"left_dp{i}", away[i - 1], lambda z, d, c, i=i: (z, d ^ i, c)).astype(F32)
    part_all = []
    for t in range(turns):
        near = parts[t][0], permute(f"parts_core{t}", parts[t][1], swap)
        part_all += [v[0] for v in near]
        for i in range(1, ndp):
            leave = after(jnp.stack([v[i] for v in near]), away)
            part_all.append(across(f"parts_dp{t}", leave, i))
    lots = []
    for t in range(turns):
        rsplit = rights[t].reshape(ndp, nseq, rk, pwidth)
        for i in range(ndp):
            lots.append(jnp.concatenate(
                [pick(grads[t], dpi ^ i, 0).reshape(nseq, -1, blk), pick(rsplit, dpi ^ i, 0).astype(BF).reshape(nseq, -1, blk)],
                axis=1,
            ))
    lots = after(lots, away)
    came = [
        permute(f"grads{t}{i}", lots[t * ndp + i], lambda z, d, c, t=t, i=i: (z ^ handled(d, c, t), d ^ i, c))
        for t in range(turns) for i in range(ndp)
    ]
    owned = sum(v.astype(F32) for v in came)
    step = npan
    while step > 1:
        step //= 2
        sent = mine[step:].astype(BF)
        mine = mine[:step] + permute(f"left_tensor{step}", sent, lambda z, d, c, k=step: (z ^ k, d, c)).astype(F32)
    left = mine[0]
    (dx,) = call(
        "dx", functools.partial(dx_kernel, dims), [SM] * 2 + [VM] * (2 + len(part_all)),
        [((toks, width), BF)], [pltpu.VMEM((toks, width), F32)],
        (pairs, live, left_t, gfac, *part_all), 12, 10**8,
    )
    owned = after(owned, dx)
    leave = pick(owned, 1 - core, 0).astype(BF)
    swapped = permute("grads_core", leave, swap)
    nblock = 2 * slots * rows
    up_sum, down_sum, right_sum, left_sum = call(
        "finish", functools.partial(finish_kernel, nblock), [VM] * 3,
        [((slots, rows, blk), F32)] * 2 + [((rk, pwidth), F32), ((rk, chunk), F32)], [],
        (pick(owned, core, 0), swapped, left), 4, 10**6,
    )
    return dx[None], up_sum[None], down_sum[None], left_sum.T, right_sum


def solution(mesh):
    return jax.shard_map(
        per_device,
        mesh=mesh,
        in_specs=(
            P(("groups", "dp", "seq"), "tensor", None),
            P(("groups", "dp", "seq"), "tensor", None),
            P("tensor", None, None, None),
            P("tensor", None, None, None),
            P(),
            P(),
            P(),
            P(None, "tensor"),
        ),
        out_specs=(
            P(("groups", "dp", "seq"), "tensor", None),
            P(("groups", "tensor"), None, ("dp", "seq"), None),
            P(("groups", "tensor"), None, ("dp", "seq"), None),
            P(("groups", "tensor"), ("dp", "seq")),
            P(("groups", "dp", "seq"), "tensor"),
        ),
        check_vma=False,
    )
```
